128 devices in a mesh: row: 16 (over z, y), col: 8 (over x, core).
Axes of the slice: x: 4, y: 4, z: 4, core: 2. Of those that a mesh axis runs over, the one named last changes fastest.
Arguments:
- matrix: float32 [2, 8192, 4, 4096], P(None, 'row', None, 'col'), may hold values from -10 to 14, as said below
- inverse_factors: float32 [2, 512, 512], replicated, may hold values from -0.05574408 to 0.05574408
Outputs:
- panels: float32 [2, 2, 8192, 512], P(None, None, 'row')
- updated: float32 [2, 8192, 4, 4096], P(None, 'row', None, 'col')
The draws below stay inside these ranges and needn't reach their ends.
Inputs may be any that keep to these rules, and one draw needn't show every extreme that they name: Read as an 16384 x 16384 matrix, matrix is symmetric.
All inputs are finite; a program needn't handle non-finite values.
Results may differ from the reference program's by a relative error of at most 0.00012.
Values sent between devices are 32-bit elements; how exact they have to be, the bound alone decides.
No kernel may reach another device: no remote copies, remote signals or barrier semaphores. Data moves between devices by JAX's collectives and lax.ppermute only.
A program may use at most 128 MiB of HBM per device.

```python
import jax
import jax.numpy as jnp
from jax import lax

NB = 512
RBD = 2
CBD = 4
M = 16384
N_ROW = 16
N_COL = 8


def draw_matrix(key, part):
    key = jax.random.fold_in(key, 7)
    first = jax.random.fold_in(key, 0)
    base = jnp.clip(jax.random.normal(first, (M, M), jnp.float32), -6.0, 6.0)
    symmetric = 0.5 * (base + base.T)
    eye = (jnp.arange(M)[:, None] == jnp.arange(M)[None, :]).astype(jnp.float32)
    full = symmetric + 4.0 * eye
    return full.reshape(RBD, N_ROW * NB, CBD, N_COL * NB)


def scatter_about(stream_key, shape, scale, limit, kind=jnp.bfloat16):
    drawn = scale * jax.random.normal(stream_key, shape, jnp.float32)
    return jnp.clip(drawn, min=-limit, max=limit).astype(kind)


def setup_inputs(seed: int = 0) -> dict:
    splits = jax.random.split(jax.random.key(seed), 3)
    matrix = draw_matrix(jax.random.fold_in(splits[2], 71), 0)
    inverse_factors = scatter_about(splits[1], (2, NB, NB), (NB ** -0.75), 0.05574408, jnp.float32)
    return {"matrix": matrix, "inverse_factors": inverse_factors}


def reference(matrix, inverse_factors):
    order = matrix.shape[0] * matrix.shape[1]
    full = matrix.reshape(order, order)
    panels = []
    for step in range(2):
        start = step * NB
        column = full[start:, start:start + NB]
        panel = jnp.dot(column, inverse_factors[step].T, precision=lax.Precision.HIGHEST)
        rest = start + NB
        lower = panel[NB:]
        update = jnp.dot(lower, lower.T, precision=lax.Precision.HIGHEST)
        full = full.at[rest:, rest:].add(-update)
        padded = jnp.concatenate([jnp.zeros((start, NB), full.dtype), panel], axis=0)
        panels.append(padded.reshape(RBD, N_ROW * NB, NB))
    return jnp.stack(panels), full.reshape(RBD, N_ROW * NB, CBD, N_COL * NB)
```

```python
import jax
import jax.numpy as jnp
from jax import lax
from jax.sharding import PartitionSpec as P

AXES = ("row", "col")
HIGH = lax.Precision.HIGH
RING = 4
MOVES = (1, -1, 2)


def place(z, y, x, c):
    return ((z % RING) * RING + y % RING) * (2 * RING) + (x % RING) * 2 + c


def pairs(target):
    found = []
    for z in range(RING):
        for y in range(RING):
            for x in range(RING):
                for c in range(2):
                    to = target(z, y, x, c)
                    if to is not None:
                        found.append((place(z, y, x, c), place(*to)))
    return found


def along_block(d, wanted=lambda z, y, x, c: True):
    def target(z, y, x, c):
        if not wanted(z, y, x, c):
            return None
        return (z, y + d, x, c) if c == 0 else (z + d, y, x, c)

    return pairs(target)


def along_part(d, wanted=lambda z, y, x, c: True):
    def target(z, y, x, c):
        if not wanted(z, y, x, c):
            return None
        return (z + d, y, x, c) if c == 0 else (z, y + d, x, c)

    return pairs(target)


def along_x(stage, extra=False):
    def target(z, y, x, c):
        sign = 1 if c == 0 else -1
        if (sign * x) % RING == stage:
            return (z, y, x + sign, c)
        if extra and x == 0 and z == 0 and (y, c) in ((1, 0), (0, 1)):
            return (z, y, -sign, c)
        return None

    return pairs(target)


def other_core(x):
    return lax.ppermute(x, AXES, pairs(lambda z, y, x, c: (z, y, x, 1 - c)))


def send(x, moves):
    return lax.ppermute(x, AXES, moves)


def choose(index, *options):
    result = options[-1]
    for i in range(len(options) - 2, -1, -1):
        result = jnp.where(index == i, options[i], result)
    return result


def dot(a, b):
    return lax.dot_general(a, b, (((1,), (0,)), ((), ())), precision=HIGH)


def dot_t(a, b):
    return lax.dot_general(a, b, (((1,), (1,)), ((), ())), precision=HIGH)


def top_row_blocks(matrix, u, v, c):
    nb = matrix.shape[1]
    part = nb // RING
    top = matrix[0]

    def column_block(k):
        return lax.dynamic_slice(top, (0, k % RING, 0), (nb, 1, nb))[:, 0, :]

    def root(z, y, x, c):
        return z == 0 and y < 2

    own = column_block(u)
    got = {d: send(column_block(u + d), along_block(d, root)) for d in MOVES}
    first = choose(u, own, got[1], got[2], got[-1])
    second = choose(u, got[-1], own, got[1], got[2])

    def quarter(d):
        both = jnp.stack([first, second])
        return lax.dynamic_slice(both, (0, ((v + d) % RING) * part, 0), (2, part, nb))

    def holder(z, y, x, c):
        return z == 0 if c == 0 else y < 2

    mine = quarter(0)
    got = {d: send(quarter(d), along_part(d, holder)) for d in MOVES}
    part_a = choose(v, mine[0], got[1][0], got[2][0], got[-1][0])
    part_b = jnp.where(
        c == 0,
        choose(v, mine[1], got[1][1], got[2][1], got[-1][1]),
        choose(v, got[-1][0], mine[0], got[1][0], got[2][0]),
    )
    piece = jnp.stack([part_a, part_b])

    got = {d: send(piece, along_part(d)) for d in MOVES}
    whole = jnp.zeros((2, RING, part, nb), matrix.dtype)
    for d, value in ((0, piece), (-1, got[1]), (1, got[-1]), (2, got[2])):
        whole = lax.dynamic_update_slice(whole, value[:, None], (0, (v + d) % RING, 0, 0))
    whole = whole.reshape(2, nb, nb)

    before = send(whole, along_block(1))
    after = send(whole, along_block(-1))
    far_a = send(before[0], along_block(1))
    far_b = send(after[1], along_block(-1))
    return whole, before, after, jnp.stack([far_a, far_b])


def row_inputs(matrix, u, v, x, c):
    nb = matrix.shape[1]
    half = nb // 2
    s = jnp.where(c == 0, x, (-x) % RING)
    chunks = []
    corner = None
    for a in range(2):
        own = matrix[a, :, 0, :]
        one = send(own, along_x(0))
        two = send(jnp.where(x == 0, own, one), along_x(1, extra=a == 0))
        three = send(two, along_x(2))
        chunks.append(choose(s, own, one, two, three))
        if a == 0:
            corner = choose(s, own, one, two, two)

    start = jnp.where(c == 0, corner[:half], corner.T[half:])

    def source(z, y, x, c):
        return z == 0 and y == 1 - c

    got = {d: send(start, along_part(d, source)) for d in MOVES}
    line = choose(v, start, got[1], got[2], got[-1])

    def spread(z, y, x, c):
        return y == 1 if c == 0 else z == 0

    got = {d: send(line, along_block(d, spread)) for d in MOVES}
    w = (u - 1 + c) % RING
    mine = choose(w, line, got[1], got[2], got[-1])
    theirs = other_core(mine)
    corner = jnp.where(c == 0, jnp.concatenate([mine, theirs]), jnp.concatenate([theirs, mine]))

    swapped = [other_core(chunk) for chunk in chunks]
    left = jnp.concatenate([jnp.where(c == 0, m, o) for m, o in zip(chunks, swapped)])
    right = jnp.concatenate([jnp.where(c == 0, o, m) for m, o in zip(chunks, swapped)])
    return left, right, corner


def body(matrix, inverse_factors):
    rbd, nb, cbd, _ = matrix.shape
    prow = lax.axis_index("row")
    pcol = lax.axis_index("col")
    z, y = prow // RING, prow % RING
    x, c = pcol // 2, pcol % 2
    u = jnp.where(c == 0, y, z)
    v = jnp.where(c == 0, z, y)

    blocks = top_row_blocks(matrix, u, v, c)
    left, right, corner = row_inputs(matrix, u, v, x, c)

    inv0, inv1 = inverse_factors[0], inverse_factors[1]
    row_block = jnp.repeat(jnp.arange(rbd, dtype=jnp.int32) * 16 + prow, nb)[:, None]
    p0 = dot_t(left, inv0)
    p01 = dot_t(corner, inv0)
    p1 = dot_t(right - dot_t(p0, p01), inv1)
    p1 = jnp.where(row_block >= 1, p1, 0.0)
    panels = jnp.stack([p0, p1]).reshape(2, rbd, nb, nb)

    z0 = jnp.where(row_block >= 1, dot(p0, inv0), 0.0)
    y1 = jnp.where(row_block >= 2, dot(p1, inv1), 0.0)
    y0 = z0 - dot(y1, dot(p01, inv0))
    general = jnp.concatenate([y0, y1], axis=1)
    only0 = jnp.concatenate([z0, jnp.zeros_like(y1)], axis=1)
    edge = jnp.where(pcol == 0, 0.0, jnp.where(pcol == 1, only0, general))

    tops = jnp.zeros((cbd, 2, nb, nb), matrix.dtype)
    for d, block in zip((0, -1, 1, 2), blocks):
        tops = lax.dynamic_update_slice(tops, block[None], ((u + d) % RING, 0, 0, 0))
    tops = tops.reshape(cbd, 2 * nb, nb)
    updates = [dot(edge if k == 0 else general, tops[k]) for k in range(cbd)]
    update = jnp.stack(updates, axis=1).reshape(rbd, nb, cbd, nb)
    return panels, matrix - update


def solution(mesh):
    return jax.shard_map(
        body,
        mesh=mesh,
        in_specs=(P(None, "row", None, "col"), P()),
        out_specs=(P(None, None, "row", None), P(None, "row", None, "col")),
        check_vma=False,
    )
```

```python
import functools

import jax
import jax.numpy as jnp
from jax import lax
from jax.experimental import pallas as pl
from jax.experimental.pallas import tpu as pltpu
from jax.sharding import PartitionSpec as P

AXES = ("row", "col")
RING = 4
MOVES = (1, -1, 2)
VMEM_BYTES = 50 * 1024 * 1024
NN = (((1,), (0,)), ((), ()))
NT = (((1,), (1,)), ((), ()))


def place(z, y, x, c):
    return ((z % RING) * RING + y % RING) * (2 * RING) + (x % RING) * 2 + c


def pairs(target):
    found = []
    for z in range(RING):
        for y in range(RING):
            for x in range(RING):
                for c in range(2):
                    to = target(z, y, x, c)
                    if to is not None:
                        found.append((place(z, y, x, c), place(*to)))
    return found


def everyone(z, y, x, c):
    return True


def along_u(d, wanted=everyone):
    def target(z, y, x, c):
        if not wanted(z, y, x, c):
            return None
        return (z, y + d, x, c) if c == 0 else (z + d, y, x, c)

    return pairs(target)


def along_v(d, wanted=everyone):
    def target(z, y, x, c):
        if not wanted(z, y, x, c):
            return None
        return (z + d, y, x, c) if c == 0 else (z, y + d, x, c)

    return pairs(target)


def send(x, moves):
    return lax.ppermute(x, AXES, moves)


def other_core(x):
    return send(x, pairs(lambda z, y, x, c: (z, y, x, 1 - c)))


def choose(index, *options):
    result = options[-1]
    for i in range(len(options) - 2, -1, -1):
        result = jnp.where(index == i, options[i], result)
    return result


def ring_order(index, own, got):
    shape = (own.shape[0], RING) + own.shape[1:]
    whole = jnp.zeros(shape, own.dtype)
    for d, value in ((0, own), (-1, got[1]), (1, got[-1]), (2, got[2])):
        start = (0, (index + d) % RING) + (0,) * (len(shape) - 2)
        whole = lax.dynamic_update_slice(whole, value[:, None], start)
    return whole.reshape((own.shape[0], RING * own.shape[1]) + own.shape[2:])


def split(x):
    high = x.astype(jnp.bfloat16)
    low = (x - high.astype(jnp.float32)).astype(jnp.bfloat16)
    return high, low


def dot3(a, b, dims):
    a_high, a_low = a
    b_high, b_low = b
    one = functools.partial(
        lax.dot_general, dimension_numbers=dims, preferred_element_type=jnp.float32
    )
    return one(a_high, b_high) + (one(a_high, b_low) + one(a_low, b_high))


def factors_kernel(
    where_ref, mine_ref, theirs_ref, corner_ref, inv_ref,
    panels_ref, yg_high, yg_low, ye_high, ye_low,
    inv_high, inv_low, p01_high, p01_low, f_high, f_low,
):
    a = pl.program_id(0)
    prow, pcol, core = where_ref[0], where_ref[1], where_ref[2]
    part = yg_high.shape[2] // 2

    @pl.when((a == 0) & (pl.program_id(1) == 0))
    def _():
        for i in range(2):
            inv_high[i], inv_low[i] = split(inv_ref[i])
        inv0 = inv_high[0], inv_low[0]
        p01 = split(dot3(split(corner_ref[...]), inv0, NT))
        p01_high[...], p01_low[...] = p01
        f_high[...], f_low[...] = split(dot3(p01, inv0, NN))

    inv0 = inv_high[0], inv_low[0]
    inv1 = inv_high[1], inv_low[1]
    mine, theirs = mine_ref[0], theirs_ref[0]
    left = jnp.where(core == 0, mine, theirs)
    right = jnp.where(core == 0, theirs, mine)
    block = a * 16 + prow
    p0 = dot3(split(left), inv0, NT)
    p0_parts = split(p0)
    below = right - dot3(p0_parts, (p01_high[...], p01_low[...]), NT)
    p1 = jnp.where(block >= 1, dot3(split(below), inv1, NT), 0.0)
    panels_ref[0, 0] = p0
    panels_ref[1, 0] = p1
    z0 = jnp.where(block >= 1, dot3(p0_parts, inv0, NN), 0.0)
    y1 = jnp.where(block >= 2, dot3(split(p1), inv1, NN), 0.0)
    y0 = z0 - dot3(split(y1), (f_high[...], f_low[...]), NN)
    e0 = jnp.where(pcol == 0, 0.0, jnp.where(pcol == 1, z0, y0))
    e1 = jnp.where(pcol <= 1, 0.0, y1)
    for high, low, first, second in ((yg_high, yg_low, y0, y1), (ye_high, ye_low, e0, e1)):
        for k in range(RING):
            for i, value in enumerate((first, second)):
                h, l = split(value[:, k * part : (k + 1) * part])
                high[k, :, i * part : (i + 1) * part] = h
                low[k, :, i * part : (i + 1) * part] = l


def row_factors(where, mine, theirs, corner, inverse_factors):
    rbd, nb, _ = mine.shape
    tile = nb // 2
    rows = pl.BlockSpec((1, tile, nb), lambda a, t: (a, t, 0))
    parts = pl.BlockSpec((RING, tile, nb // 2), lambda a, t: (0, a * 2 + t, 0))
    parts_shape = jax.ShapeDtypeStruct((RING, rbd * nb, nb // 2), jnp.bfloat16)
    half = pltpu.VMEM((nb, nb), jnp.bfloat16)
    return pl.pallas_call(
        factors_kernel,
        grid=(rbd, 2),
        in_specs=[
            pl.BlockSpec(memory_space=pltpu.SMEM),
            rows,
            rows,
            pl.BlockSpec((nb, nb), lambda a, t: (0, 0)),
            pl.BlockSpec((2, nb, nb), lambda a, t: (0, 0, 0)),
        ],
        out_specs=[pl.BlockSpec((2, 1, tile, nb), lambda a, t: (0, a, t, 0))] + [parts] * 4,
        out_shape=[jax.ShapeDtypeStruct((2, rbd, nb, nb), jnp.float32)] + [parts_shape] * 4,
        scratch_shapes=[pltpu.VMEM((2, nb, nb), jnp.bfloat16)] * 2 + [half] * 4,
        compiler_params=pltpu.CompilerParams(vmem_limit_bytes=VMEM_BYTES),
        cost_estimate=pl.CostEstimate(flops=20 * 10**9, bytes_accessed=24 * 2**20, transcendentals=0),
    )(where, mine, theirs, corner, inverse_factors)


def update_kernel(count, ks_ref, x_ref, yg_high, yg_low, ye_high, ye_low, *rest):
    pieces, out_ref, rhs = rest[:count], rest[count], rest[count + 1]
    rows = yg_high.shape[1]
    depth = yg_high.shape[2]
    cbd = rhs.shape[0]
    lanes = rhs.shape[2] // RING
    stride = RING * cbd

    @pl.when((pl.program_id(0) == 0) & (pl.program_id(1) == 0))
    def _():
        for j in range(count):
            for c in range(cbd):
                for t in range(RING):
                    high, low = split(pieces[j][pl.ds(t * cbd + c, depth, stride=stride), :])
                    for place_at, value in ((0, high), (1, low), (2, high)):
                        start = (3 * j + place_at) * depth
                        rhs[c, start : start + depth, t * lanes : (t + 1) * lanes] = value

    left = []
    for high, low in ((ye_high, ye_low), (yg_high, yg_low)):
        terms = []
        for j in range(count):
            h, l = high[ks_ref[j]], low[ks_ref[j]]
            terms += [h, h, l]
        left.append(jnp.concatenate(terms, axis=1))
    for c in range(cbd):
        product = jnp.dot(left[min(c, 1)], rhs[c], preferred_element_type=jnp.float32)
        for t in range(RING):
            at = pl.ds(t * cbd + c, rows, stride=stride)
            out_ref[at, :] = x_ref[at, :] - product[:, t * lanes : (t + 1) * lanes]


def subtract_products(lines, factors, ks, pieces, cbd):
    nb = 2 * factors[0].shape[2]
    rbd = factors[0].shape[1] // nb
    count = len(pieces)
    tile = nb // 2
    block = pl.BlockSpec((tile * RING * cbd, lines.shape[1]), lambda a, t: (a * 2 + t, 0))
    parts = pl.BlockSpec((RING, tile, nb // 2), lambda a, t: (0, a * 2 + t, 0))
    whole = pl.BlockSpec(
        pieces[0].shape, lambda a, t: (0, 0), pipeline_mode=pl.Buffered(buffer_count=1)
    )
    return pl.pallas_call(
        functools.partial(update_kernel, count),
        grid=(rbd, 2),
        in_specs=[pl.BlockSpec(memory_space=pltpu.SMEM), block] + [parts] * 4 + [whole] * count,
        out_specs=block,
        out_shape=jax.ShapeDtypeStruct(lines.shape, lines.dtype),
        scratch_shapes=[pltpu.VMEM((cbd, 3 * count * (nb // 2), nb), jnp.bfloat16)],
        compiler_params=pltpu.CompilerParams(vmem_limit_bytes=VMEM_BYTES),
        cost_estimate=pl.CostEstimate(
            flops=3 * count * 11 * 10**8, bytes_accessed=(16 + 4 + 2 * count) * 2**20, transcendentals=0
        ),
    )(ks, lines, *factors, *pieces)


def column_kernel(x_ref, out_ref):
    rows, nb = out_ref.shape[1:]
    lanes = nb // RING
    cbd = x_ref.shape[0] // rows // RING
    for t in range(RING):
        at = pl.ds(t * cbd, rows, stride=RING * cbd)
        out_ref[0, :, t * lanes : (t + 1) * lanes] = x_ref[at, :]


def first_column(lines, rbd, nb, cbd):
    tile = nb // 2
    return pl.pallas_call(
        column_kernel,
        grid=(rbd, 2),
        in_specs=[pl.BlockSpec((tile * RING * cbd, lines.shape[1]), lambda a, t: (a * 2 + t, 0))],
        out_specs=pl.BlockSpec((1, tile, nb), lambda a, t: (a, t, 0)),
        out_shape=jax.ShapeDtypeStruct((rbd, nb, nb), lines.dtype),
        cost_estimate=pl.CostEstimate(flops=0, bytes_accessed=10 * 2**20, transcendentals=0),
    )(lines)


def corner_kernel(core_ref, x_ref, out_ref):
    half, nb = out_ref.shape
    lanes = nb // RING
    cbd = x_ref.shape[0] // nb // RING
    stride = RING * cbd

    @pl.when(core_ref[0] == 0)
    def _():
        for t in range(RING):
            out_ref[:, t * lanes : (t + 1) * lanes] = x_ref[pl.ds(t * cbd, half, stride=stride), :]

    @pl.when(core_ref[0] != 0)
    def _():
        for t in range(RING // 2):
            at = pl.ds((t + RING // 2) * cbd, nb, stride=stride)
            out_ref[t * lanes : (t + 1) * lanes, :] = x_ref[at, :].T


def corner_half(core, lines, nb, cbd):
    return pl.pallas_call(
        corner_kernel,
        grid=(1,),
        in_specs=[
            pl.BlockSpec(memory_space=pltpu.SMEM),
            pl.BlockSpec((nb * RING * cbd, lines.shape[1]), lambda i: (0, 0)),
        ],
        out_specs=pl.BlockSpec((nb // 2, nb), lambda i: (0, 0)),
        out_shape=jax.ShapeDtypeStruct((nb // 2, nb), lines.dtype),
        compiler_params=pltpu.CompilerParams(vmem_limit_bytes=VMEM_BYTES),
        cost_estimate=pl.CostEstimate(flops=0, bytes_accessed=5 * 2**20, transcendentals=0),
    )(core, lines)


def to_lines(matrix):
    rbd, rows, cbd, nb = matrix.shape
    cut = matrix.reshape(rbd, rows, cbd, RING, nb // RING)
    return cut.transpose(0, 1, 3, 2, 4).reshape(-1, nb // RING)


def from_lines(lines, shape):
    rbd, rows, cbd, nb = shape
    cut = lines.reshape(rbd, rows, RING, cbd, nb // RING)
    return cut.transpose(0, 1, 3, 2, 4).reshape(shape)


def share(x, index, first, second):
    one = send(x, first)
    two = send(jnp.where(index == 0, x, one), second)
    return choose(index, x, one, two, two)


def top_rows(lines, u, v, c):
    part = lines.shape[0] // 2 // RING
    small = part // RING

    def rows(k):
        return lax.dynamic_slice_in_dim(lines, (k % RING) * part, part)

    def root(z, y, x, c):
        return z == 0 and y < 2

    got = {d: send(rows(u + d), along_u(d, root)) for d in MOVES}
    own = rows(u)

    def quarter(d):
        begin = ((v + d) % RING) * small
        o, p, q, m = (
            lax.dynamic_slice_in_dim(t, begin, small) for t in (own, got[1], got[2], got[-1])
        )
        return jnp.stack([choose(u, o, p, q, m), choose(u, m, o, p, q)])

    def holder(z, y, x, c):
        return z == 0 if c == 0 else y < 2

    mine = quarter(0)
    sent = {d: send(quarter(d), along_v(d, holder)) for d in MOVES}
    part_a = choose(v, mine[0], sent[1][0], sent[2][0], sent[-1][0])
    part_b = jnp.where(
        c == 0,
        choose(v, mine[1], sent[1][1], sent[2][1], sent[-1][1]),
        choose(v, sent[-1][0], mine[0], sent[1][0], sent[2][0]),
    )
    piece = jnp.stack([part_a, part_b])
    whole = ring_order(v, piece, {d: send(piece, along_v(d)) for d in MOVES})

    before = send(whole, along_u(1))
    after = send(whole, along_u(-1))
    far_a = send(before[0], along_u(1))
    far_b = send(after[1], along_u(-1))
    far = jnp.concatenate([far_a, far_b])
    lanes = lines.shape[1]
    return [t.reshape(-1, lanes) for t in (whole, before, after, far)]


def row_inputs(column, start, u, v, x, c):
    def sign(c):
        return 1 if c == 0 else -1

    def x_first(z, y, x, c):
        return (z, y, sign(c), c) if x == 0 else None

    def x_second(z, y, x, c):
        if x == 0:
            return (z, y, -sign(c), c)
        return (z, y, 2, c) if x == sign(c) % RING else None

    s = jnp.where(c == 0, x, -x) % RING
    start = share(start, s, pairs(x_first), pairs(x_second))
    mine = share(column, s, pairs(x_first), pairs(x_second))
    theirs = other_core(mine)

    def uv(z, y, c):
        return (y, z) if c == 0 else (z, y)

    def zyxc(u, v, x, c):
        return (v, u, x, c) if c == 0 else (u, v, x, c)

    def v_first(z, y, x, c):
        u, v = uv(z, y, c)
        return zyxc(u, 1, x, c) if v == 0 and u == 1 - c else None

    def v_second(z, y, x, c):
        u, v = uv(z, y, c)
        return zyxc(u, 3 if v == 0 else 2, x, c) if v < 2 and u == 1 - c else None

    def u_first(z, y, x, c):
        u, v = uv(z, y, c)
        return zyxc(u + 1, v, x, c) if u == 1 - c else None

    def u_second(z, y, x, c):
        u, v = uv(z, y, c)
        w = (u - 1 + c) % RING
        return zyxc(u - 1 if w == 0 else u + 1, v, x, c) if w < 2 else None

    line = share(start, v, pairs(v_first), pairs(v_second))
    here = share(line, (u - 1 + c) % RING, pairs(u_first), pairs(u_second))
    there = other_core(here)
    corner = jnp.concatenate([jnp.where(c == 0, here, there), jnp.where(c == 0, there, here)])
    return mine, theirs, corner


def body(matrix, inverse_factors):
    rbd, nb, cbd, _ = matrix.shape
    prow = lax.axis_index("row")
    pcol = lax.axis_index("col")
    z, y = prow // RING, prow % RING
    x, c = pcol // 2, pcol % 2
    u = jnp.where(c == 0, y, z)
    v = jnp.where(c == 0, z, y)

    lines = to_lines(matrix)
    own, before, after, far = top_rows(lines, u, v, c)
    start = corner_half(c.astype(jnp.int32)[None], lines, nb, cbd)
    mine, theirs, corner = row_inputs(first_column(lines, rbd, nb, cbd), start, u, v, x, c)

    where = jnp.stack([prow, pcol, c]).astype(jnp.int32)
    panels, *factors = row_factors(where, mine, theirs, corner, inverse_factors)
    ks = jnp.stack([u, u - 1, u + 1, u + 2]).astype(jnp.int32) % RING
    partial = subtract_products(lines, factors, ks[:3], (own, before, after), cbd)
    final = subtract_products(partial, factors, ks[3:], (far,), cbd)
    return panels, from_lines(final, matrix.shape)


def solution(mesh):
    return jax.shard_map(
        body,
        mesh=mesh,
        in_specs=(P(None, "row", None, "col"), P()),
        out_specs=(P(None, None, "row", None), P(None, "row", None, "col")),
        check_vma=False,
    )
```

```python
import functools

import jax
import jax.numpy as jnp
from jax import lax
from jax.experimental import pallas as pl
from jax.experimental.pallas import tpu as pltpu
from jax.sharding import PartitionSpec as P

AXES = ("row", "col")
RING = 4
MOVES = (1, -1, 2)
SPLIT = 2
VMEM_BYTES = 50 * 1024 * 1024


def place(z, y, x, c):
    return ((z % RING) * RING + y % RING) * (2 * RING) + (x % RING) * 2 + c


def pairs(target):
    found = []
    for z in range(RING):
        for y in range(RING):
            for x in range(RING):
                for c in range(2):
                    to = target(z, y, x, c)
                    if to is not None:
                        found.append((place(z, y, x, c), place(*to)))
    return found


def everyone(z, y, x, c):
    return True


def along_u(d, wanted=everyone):
    def target(z, y, x, c):
        if not wanted(z, y, x, c):
            return None
        return (z, y + d, x, c) if c == 0 else (z + d, y, x, c)

    return pairs(target)


def along_v(d, wanted=everyone):
    def target(z, y, x, c):
        if not wanted(z, y, x, c):
            return None
        return (z + d, y, x, c) if c == 0 else (z, y + d, x, c)

    return pairs(target)


def send(x, moves):
    return lax.ppermute(x, AXES, moves)


def other_core(x):
    return send(x, pairs(lambda z, y, x, c: (z, y, x, 1 - c)))


def choose(index, *options):
    result = options[-1]
    for i in range(len(options) - 2, -1, -1):
        result = jnp.where(index == i, options[i], result)
    return result


def ring_order(index, own, got):
    shape = (own.shape[0], RING) + own.shape[1:]
    whole = jnp.zeros(shape, own.dtype)
    for d, value in ((0, own), (-1, got[1]), (1, got[-1]), (2, got[2])):
        start = (0, (index + d) % RING) + (0,) * (len(shape) - 2)
        whole = lax.dynamic_update_slice(whole, value[:, None], start)
    return whole.reshape((own.shape[0], RING * own.shape[1]) + own.shape[2:])


def split(x):
    high = x.astype(jnp.bfloat16)
    low = (x - high.astype(jnp.float32)).astype(jnp.bfloat16)
    return high, low


def stack_left(x):
    high, low = split(x)
    return jnp.concatenate([high, high, low], axis=1)


def put_right(ref, columns, x):
    high, low = split(x)
    depth = x.shape[0]
    for i, value in enumerate((high, low, high)):
        ref[i * depth : (i + 1) * depth, columns] = value


def dot(a, b):
    return jnp.dot(a, b, preferred_element_type=jnp.float32)


def weights_kernel(inv_ref, first_ref, second_ref, right):
    nb = inv_ref.shape[1]
    for i, out_ref in enumerate((first_ref, second_ref)):
        inv = inv_ref[i]
        turned = inv.T
        put_right(right, slice(None), inv)
        put_right(out_ref, slice(0, nb), turned)
        put_right(out_ref, slice(nb, 2 * nb), dot(stack_left(turned), right[...]))


def weights(inverse_factors):
    _, nb, _ = inverse_factors.shape
    return pl.pallas_call(
        weights_kernel,
        out_shape=[jax.ShapeDtypeStruct((3 * nb, 2 * nb), jnp.bfloat16)] * 2,
        scratch_shapes=[pltpu.VMEM((3 * nb, nb), jnp.bfloat16)],
        compiler_params=pltpu.CompilerParams(vmem_limit_bytes=VMEM_BYTES),
        cost_estimate=pl.CostEstimate(flops=2 * 10**9, bytes_accessed=8 * 2**20, transcendentals=0),
    )(inverse_factors)


def factors_kernel(
    where_ref, mine_ref, theirs_ref, corner_ref, first_ref, second_ref,
    panels_ref, yg_high, yg_low, ye_high, ye_low,
    f_turned, f_right,
):
    a = pl.program_id(0)
    prow, pcol, core = where_ref[0], where_ref[1], where_ref[2]
    part = yg_high.shape[2] // 2
    nb = mine_ref.shape[2]

    @pl.when((a == 0) & (pl.program_id(1) == 0))
    def _():
        f = dot(stack_left(corner_ref[...]), first_ref[:, nb:])
        put_right(f_right, slice(None), f)
        put_right(f_turned, slice(None), f.T)

    mine, theirs = mine_ref[0], theirs_ref[0]
    left = stack_left(jnp.where(core == 0, mine, theirs))
    right = jnp.where(core == 0, theirs, mine)
    block = a * 16 + prow
    panels_ref[0, 0] = dot(left, first_ref[:, :nb])
    z0 = jnp.where(block >= 1, dot(left, first_ref[:, nb:]), 0.0)
    below = stack_left(right - dot(left, f_turned[...]))
    panels_ref[1, 0] = jnp.where(block >= 1, dot(below, second_ref[:, :nb]), 0.0)
    y1 = jnp.where(block >= 2, dot(below, second_ref[:, nb:]), 0.0)
    y0 = z0 - dot(stack_left(y1), f_right[...])
    e0 = jnp.where(pcol == 0, 0.0, jnp.where(pcol == 1, z0, y0))
    e1 = jnp.where(pcol <= 1, 0.0, y1)
    for high, low, first, second in ((yg_high, yg_low, y0, y1), (ye_high, ye_low, e0, e1)):
        for i, value in enumerate((first, second)):
            h, l = split(value)
            for k in range(RING):
                high[k, :, i * part : (i + 1) * part] = h[:, k * part : (k + 1) * part]
                low[k, :, i * part : (i + 1) * part] = l[:, k * part : (k + 1) * part]


def row_factors(where, mine, theirs, corner, first, second):
    rbd, nb, _ = mine.shape
    tile = nb // SPLIT
    rows = pl.BlockSpec((1, tile, nb), lambda a, t: (a, t, 0))
    parts = pl.BlockSpec((RING, tile, nb // 2), lambda a, t: (0, a * SPLIT + t, 0))
    parts_shape = jax.ShapeDtypeStruct((RING, rbd * nb, nb // 2), jnp.bfloat16)
    fixed = [
        pl.BlockSpec(x.shape, lambda a, t: (0, 0), pipeline_mode=pl.Buffered(buffer_count=1))
        for x in (corner, first, second)
    ]
    return pl.pallas_call(
        factors_kernel,
        grid=(rbd, SPLIT),
        in_specs=[pl.BlockSpec(memory_space=pltpu.SMEM), rows, rows] + fixed,
        out_specs=[pl.BlockSpec((2, 1, tile, nb), lambda a, t: (0, a, t, 0))] + [parts] * 4,
        out_shape=[jax.ShapeDtypeStruct((2, rbd, nb, nb), jnp.float32)] + [parts_shape] * 4,
        scratch_shapes=[pltpu.VMEM((3 * nb, nb), jnp.bfloat16)] * 2,
        compiler_params=pltpu.CompilerParams(vmem_limit_bytes=VMEM_BYTES),
        cost_estimate=pl.CostEstimate(flops=11 * 10**9, bytes_accessed=24 * 2**20, transcendentals=0),
    )(where, mine, theirs, corner, first, second)


def update_kernel(count, ks_ref, x_ref, *rest):
    factors, halves = rest[: 4 * count], rest[4 * count : 6 * count]
    out_ref, rhs = rest[6 * count], rest[6 * count + 1]
    rows, depth = factors[0].shape[1:]
    half = depth // 2
    cbd = rhs.shape[0]
    lanes = rhs.shape[2] // RING
    stride = RING * cbd

    @pl.when((pl.program_id(0) == 0) & (pl.program_id(1) == 0))
    def _():
        for j in range(2 * count):
            for c in range(cbd):
                for t in range(RING):
                    high, low = split(halves[j][pl.ds(t * cbd + c, half, stride=stride), :])
                    for place_at, value in ((0, high), (1, low), (2, high)):
                        start = (3 * (j // 2) + place_at) * depth + (j % 2) * half
                        rhs[c, start : start + half, t * lanes : (t + 1) * lanes] = value

    left = []
    for kind in (1, 0):
        terms = []
        for j in range(count):
            h, l = factors[4 * j + 2 * kind][0], factors[4 * j + 2 * kind + 1][0]
            terms += [h, h, l]
        left.append(jnp.concatenate(terms, axis=1))
    for c in range(cbd):
        product = dot(left[min(c, 1)], rhs[c])
        for t in range(RING):
            at = pl.ds(t * cbd + c, rows, stride=stride)
            out_ref[at, :] = x_ref[at, :] - product[:, t * lanes : (t + 1) * lanes]


def subtract_products(lines, factors, ks, halves, cbd):
    nb = 2 * factors[0].shape[2]
    rbd = factors[0].shape[1] // nb
    count = len(halves) // 2
    tile = nb // SPLIT
    block = pl.BlockSpec((tile * RING * cbd, lines.shape[1]), lambda a, t, ks: (a * SPLIT + t, 0))
    parts = [
        pl.BlockSpec((1, tile, nb // 2), lambda a, t, ks, j=j: (ks[j], a * SPLIT + t, 0))
        for j in range(count)
        for _ in factors
    ]
    whole = [
        pl.BlockSpec(
            (nb // RING * RING * cbd, lines.shape[1]),
            lambda a, t, ks, i=i: (i, 0),
            pipeline_mode=pl.Buffered(buffer_count=1),
        )
        for _, i in halves
    ]
    return pl.pallas_call(
        functools.partial(update_kernel, count),
        grid_spec=pltpu.PrefetchScalarGridSpec(
            num_scalar_prefetch=1,
            grid=(rbd, SPLIT),
            in_specs=[block] + parts + whole,
            out_specs=block,
            scratch_shapes=[pltpu.VMEM((cbd, 3 * count * (nb // 2), nb), jnp.bfloat16)],
        ),
        out_shape=jax.ShapeDtypeStruct(lines.shape, lines.dtype),
        compiler_params=pltpu.CompilerParams(vmem_limit_bytes=VMEM_BYTES),
        cost_estimate=pl.CostEstimate(
            flops=3 * count * 11 * 10**8, bytes_accessed=(16 + 4 * count) * 2**20, transcendentals=0
        ),
    )(ks, lines, *(factors * count), *(t for t, _ in halves))


def column_kernel(x_ref, out_ref):
    rows, nb = out_ref.shape[1:]
    lanes = nb // RING
    cbd = x_ref.shape[0] // rows // RING
    for t in range(RING):
        at = pl.ds(t * cbd, rows, stride=RING * cbd)
        out_ref[0, :, t * lanes : (t + 1) * lanes] = x_ref[at, :]


def first_column(lines, rbd, nb, cbd):
    tile = nb // 2
    return pl.pallas_call(
        column_kernel,
        grid=(rbd, 2),
        in_specs=[pl.BlockSpec((tile * RING * cbd, lines.shape[1]), lambda a, t: (a * 2 + t, 0))],
        out_specs=pl.BlockSpec((1, tile, nb), lambda a, t: (a, t, 0)),
        out_shape=jax.ShapeDtypeStruct((rbd, nb, nb), lines.dtype),
        cost_estimate=pl.CostEstimate(flops=0, bytes_accessed=10 * 2**20, transcendentals=0),
    )(lines)


def corner_kernel(core_ref, x_ref, out_ref):
    half, nb = out_ref.shape
    lanes = nb // RING
    cbd = x_ref.shape[0] // nb // RING
    stride = RING * cbd

    @pl.when(core_ref[0] == 0)
    def _():
        for t in range(RING):
            out_ref[:, t * lanes : (t + 1) * lanes] = x_ref[pl.ds(t * cbd, half, stride=stride), :]

    @pl.when(core_ref[0] != 0)
    def _():
        for t in range(RING // 2):
            at = pl.ds((t + RING // 2) * cbd, nb, stride=stride)
            out_ref[t * lanes : (t + 1) * lanes, :] = x_ref[at, :].T


def corner_half(core, lines, nb, cbd):
    return pl.pallas_call(
        corner_kernel,
        grid=(1,),
        in_specs=[
            pl.BlockSpec(memory_space=pltpu.SMEM),
            pl.BlockSpec((nb * RING * cbd, lines.shape[1]), lambda i: (0, 0)),
        ],
        out_specs=pl.BlockSpec((nb // 2, nb), lambda i: (0, 0)),
        out_shape=jax.ShapeDtypeStruct((nb // 2, nb), lines.dtype),
        compiler_params=pltpu.CompilerParams(vmem_limit_bytes=VMEM_BYTES),
        cost_estimate=pl.CostEstimate(flops=0, bytes_accessed=5 * 2**20, transcendentals=0),
    )(core, lines)


def to_lines(matrix):
    rbd, rows, cbd, nb = matrix.shape
    cut = matrix.reshape(rbd, rows, cbd, RING, nb // RING)
    return cut.transpose(0, 1, 3, 2, 4).reshape(-1, nb // RING)


def from_lines(lines, shape):
    rbd, rows, cbd, nb = shape
    cut = lines.reshape(rbd, rows, RING, cbd, nb // RING)
    return cut.transpose(0, 1, 3, 2, 4).reshape(shape)


def share(x, index, first, second):
    one = send(x, first)
    two = send(jnp.where(index == 0, x, one), second)
    return choose(index, x, one, two, two)


def top_rows(lines, u, v, c):
    part = lines.shape[0] // 2 // RING
    small = part // RING

    def rows(k):
        return lax.dynamic_slice_in_dim(lines, (k % RING) * part, part)

    def root(z, y, x, c):
        return z == 0 and y < 2

    got = {d: send(rows(u + d), along_u(d, root)) for d in MOVES}
    own = rows(u)

    def quarter(d):
        begin = ((v + d) % RING) * small
        o, p, q, m = (
            lax.dynamic_slice_in_dim(t, begin, small) for t in (own, got[1], got[2], got[-1])
        )
        return jnp.stack([choose(u, o, p, q, m), choose(u, m, o, p, q)])

    def holder(z, y, x, c):
        return z == 0 if c == 0 else y < 2

    mine = quarter(0)
    sent = {d: send(quarter(d), along_v(d, holder)) for d in MOVES}
    part_a = choose(v, mine[0], sent[1][0], sent[2][0], sent[-1][0])
    part_b = jnp.where(
        c == 0,
        choose(v, mine[1], sent[1][1], sent[2][1], sent[-1][1]),
        choose(v, sent[-1][0], mine[0], sent[1][0], sent[2][0]),
    )
    piece = jnp.stack([part_a, part_b])
    whole = ring_order(v, piece, {d: send(piece, along_v(d)) for d in MOVES})

    before = send(whole, along_u(1))
    after = send(whole, along_u(-1))
    return whole, before, after


def row_inputs(column, start, u, v, x, c):
    def sign(c):
        return 1 if c == 0 else -1

    def x_first(z, y, x, c):
        return (z, y, sign(c), c) if x == 0 else None

    def x_second(z, y, x, c):
        if x == 0:
            return (z, y, -sign(c), c)
        return (z, y, 2, c) if x == sign(c) % RING else None

    s = jnp.where(c == 0, x, -x) % RING
    start = share(start, s, pairs(x_first), pairs(x_second))
    mine = share(column, s, pairs(x_first), pairs(x_second))
    def uv(z, y, c):
        return (y, z) if c == 0 else (z, y)

    def zyxc(u, v, x, c):
        return (v, u, x, c) if c == 0 else (u, v, x, c)

    def v_first(z, y, x, c):
        u, v = uv(z, y, c)
        return zyxc(u, 1, x, c) if v == 0 and u == 1 - c else None

    def v_second(z, y, x, c):
        u, v = uv(z, y, c)
        return zyxc(u, 3 if v == 0 else 2, x, c) if v < 2 and u == 1 - c else None

    def u_first(z, y, x, c):
        u, v = uv(z, y, c)
        return zyxc(u + 1, v, x, c) if u == 1 - c else None

    def u_second(z, y, x, c):
        u, v = uv(z, y, c)
        w = (u - 1 + c) % RING
        return zyxc(u - 1 if w == 0 else u + 1, v, x, c) if w < 2 else None

    line = share(start, v, pairs(v_first), pairs(v_second))
    here = share(line, (u - 1 + c) % RING, pairs(u_first), pairs(u_second))
    there = other_core(here)
    corner = jnp.concatenate([jnp.where(c == 0, here, there), jnp.where(c == 0, there, here)])
    return mine, corner


def body(matrix, inverse_factors):
    rbd, nb, cbd, _ = matrix.shape
    prow = lax.axis_index("row")
    pcol = lax.axis_index("col")
    z, y = prow // RING, prow % RING
    x, c = pcol // 2, pcol % 2
    u = jnp.where(c == 0, y, z)
    v = jnp.where(c == 0, z, y)

    lines = to_lines(matrix)
    own, before, after = top_rows(lines, u, v, c)
    start = corner_half(c.astype(jnp.int32)[None], lines, nb, cbd)
    mine, corner = row_inputs(first_column(lines, rbd, nb, cbd), start, u, v, x, c)
    before, after, mine, turned = lax.optimization_barrier(
        (before, after, mine, weights(inverse_factors))
    )
    far = send(before[0], along_u(1)), send(after[1], along_u(-1))
    theirs = other_core(mine)

    where = jnp.stack([prow, pcol, c]).astype(jnp.int32)
    panels, *factors = row_factors(where, mine, theirs, corner, *turned)
    ks = jnp.stack([u, u - 1, u + 1, u + 2]).astype(jnp.int32) % RING
    far, factors = lax.optimization_barrier((far, factors))
    halves = [(t.reshape(-1, lines.shape[1]), i) for t in (own, before, after) for i in range(2)]
    halves += [(t, 0) for t in far]
    final = subtract_products(lines, factors, ks, halves, cbd)
    return panels, from_lines(final, matrix.shape)


def solution(mesh):
    return jax.shard_map(
        body,
        mesh=mesh,
        in_specs=(P(None, "row", None, "col"), P()),
        out_specs=(P(None, None, "row", None), P(None, "row", None, "col")),
        check_vma=False,
    )
```

```python
import functools

import jax
import jax.numpy as jnp
from jax import lax
from jax.experimental import pallas as pl
from jax.experimental.pallas import tpu as pltpu
from jax.sharding import PartitionSpec as P

AXES = ("row", "col")
RING = 4
MOVES = (1, -1, 2)
SPLIT = 2
VMEM_BYTES = 40 * 1024 * 1024


def place(z, y, x, c):
    return ((z % RING) * RING + y % RING) * (2 * RING) + (x % RING) * 2 + c


def pairs(target):
    found = []
    for z in range(RING):
        for y in range(RING):
            for x in range(RING):
                for c in range(2):
                    to = target(z, y, x, c)
                    if to is not None:
                        found.append((place(z, y, x, c), place(*to)))
    return found


def everyone(z, y, x, c):
    return True


def along_u(d, wanted=everyone):
    def target(z, y, x, c):
        if not wanted(z, y, x, c):
            return None
        return (z, y + d, x, c) if c == 0 else (z + d, y, x, c)

    return pairs(target)


def along_v(d, wanted=everyone):
    def target(z, y, x, c):
        if not wanted(z, y, x, c):
            return None
        return (z + d, y, x, c) if c == 0 else (z, y + d, x, c)

    return pairs(target)


def send(x, moves):
    return lax.ppermute(x, AXES, moves)


def other_core(x):
    return send(x, pairs(lambda z, y, x, c: (z, y, x, 1 - c)))


def choose(index, *options):
    result = options[-1]
    for i in range(len(options) - 2, -1, -1):
        result = jnp.where(index == i, options[i], result)
    return result


def ring_order(index, own, got):
    shape = (own.shape[0], RING) + own.shape[1:]
    whole = jnp.zeros(shape, own.dtype)
    for d, value in ((0, own), (-1, got[1]), (1, got[-1]), (2, got[2])):
        start = (0, (index + d) % RING) + (0,) * (len(shape) - 2)
        whole = lax.dynamic_update_slice(whole, value[:, None], start)
    return whole.reshape((own.shape[0], RING * own.shape[1]) + own.shape[2:])


def split(x):
    high = x.astype(jnp.bfloat16)
    low = (x - high.astype(jnp.float32)).astype(jnp.bfloat16)
    return high, low


def stack_left(x):
    high, low = split(x)
    return jnp.concatenate([high, high, low], axis=1)


def put_right(ref, columns, x):
    high, low = split(x)
    depth = x.shape[0]
    for i, value in enumerate((high, low, high)):
        ref[i * depth : (i + 1) * depth, columns] = value


def dot(a, b):
    return jnp.dot(a, b, preferred_element_type=jnp.float32)


def weights_kernel(inv_ref, first_ref, second_ref, right):
    nb = inv_ref.shape[1]
    for i, out_ref in enumerate((first_ref, second_ref)):
        inv = inv_ref[i]
        turned = inv.T
        put_right(right, slice(None), inv)
        put_right(out_ref, slice(0, nb), turned)
        put_right(out_ref, slice(nb, 2 * nb), dot(stack_left(turned), right[...]))


def weights(inverse_factors):
    _, nb, _ = inverse_factors.shape
    return pl.pallas_call(
        weights_kernel,
        out_shape=[jax.ShapeDtypeStruct((3 * nb, 2 * nb), jnp.bfloat16)] * 2,
        scratch_shapes=[pltpu.VMEM((3 * nb, nb), jnp.bfloat16)],
        compiler_params=pltpu.CompilerParams(vmem_limit_bytes=VMEM_BYTES),
        cost_estimate=pl.CostEstimate(flops=2 * 10**9, bytes_accessed=8 * 2**20, transcendentals=0),
    )(inverse_factors)


def factors_kernel(
    where_ref, mine_ref, theirs_ref, corner_ref, first_ref, second_ref,
    panels_ref, yg_high, yg_low, ye_high, ye_low,
    f_turned, f_right,
):
    a = pl.program_id(0)
    prow, pcol, core = where_ref[0], where_ref[1], where_ref[2]
    part = yg_high.shape[2] // 2
    nb = mine_ref.shape[2]

    @pl.when((a == 0) & (pl.program_id(1) == 0))
    def _():
        f = dot(stack_left(corner_ref[...]), first_ref[:, nb:])
        put_right(f_right, slice(None), f)
        put_right(f_turned, slice(None), f.T)

    mine, theirs = mine_ref[0], theirs_ref[0]
    left = stack_left(jnp.where(core == 0, mine, theirs))
    right = jnp.where(core == 0, theirs, mine)
    block = a * 16 + prow
    panels_ref[0, 0] = dot(left, first_ref[:, :nb])
    z0 = jnp.where(block >= 1, dot(left, first_ref[:, nb:]), 0.0)
    below = stack_left(right - dot(left, f_turned[...]))
    panels_ref[1, 0] = jnp.where(block >= 1, dot(below, second_ref[:, :nb]), 0.0)
    y1 = jnp.where(block >= 2, dot(below, second_ref[:, nb:]), 0.0)
    y0 = z0 - dot(stack_left(y1), f_right[...])
    e0 = jnp.where(pcol == 0, 0.0, jnp.where(pcol == 1, z0, y0))
    e1 = jnp.where(pcol <= 1, 0.0, y1)
    for high, low, first, second in ((yg_high, yg_low, y0, y1), (ye_high, ye_low, e0, e1)):
        for i, value in enumerate((first, second)):
            h, l = split(value)
            for k in range(RING):
                high[k, :, i * part : (i + 1) * part] = h[:, k * part : (k + 1) * part]
                low[k, :, i * part : (i + 1) * part] = l[:, k * part : (k + 1) * part]


def row_factors(where, mine, theirs, corner, first, second):
    rbd, nb, _ = mine.shape
    tile = nb // SPLIT
    rows = pl.BlockSpec((1, tile, nb), lambda a, t: (a, t, 0))
    parts = pl.BlockSpec((RING, tile, nb // 2), lambda a, t: (0, a * SPLIT + t, 0))
    parts_shape = jax.ShapeDtypeStruct((RING, rbd * nb, nb // 2), jnp.bfloat16)
    fixed = [
        pl.BlockSpec(x.shape, lambda a, t: (0, 0), pipeline_mode=pl.Buffered(buffer_count=1))
        for x in (corner, first, second)
    ]
    return pl.pallas_call(
        factors_kernel,
        grid=(rbd, SPLIT),
        in_specs=[pl.BlockSpec(memory_space=pltpu.SMEM), rows, rows] + fixed,
        out_specs=[pl.BlockSpec((2, 1, tile, nb), lambda a, t: (0, a, t, 0))] + [parts] * 4,
        out_shape=[jax.ShapeDtypeStruct((2, rbd, nb, nb), jnp.float32)] + [parts_shape] * 4,
        scratch_shapes=[pltpu.VMEM((3 * nb, nb), jnp.bfloat16)] * 2,
        compiler_params=pltpu.CompilerParams(vmem_limit_bytes=VMEM_BYTES),
        cost_estimate=pl.CostEstimate(flops=11 * 10**9, bytes_accessed=24 * 2**20, transcendentals=0),
    )(where, mine, theirs, corner, first, second)


def update_kernel(count, ks_ref, x_ref, *rest):
    factors, halves = rest[: 4 * count], rest[4 * count : 6 * count]
    out_ref, rhs = rest[6 * count], rest[6 * count + 1]
    rows, depth = factors[0].shape[1:]
    half = depth // 2
    cbd = rhs.shape[0]
    lanes = rhs.shape[2] // RING
    stride = RING * cbd

    left = []
    for kind in (1, 0):
        terms = []
        for j in range(count):
            h, l = factors[4 * j + 2 * kind][0], factors[4 * j + 2 * kind + 1][0]
            terms += [h, h, l]
        left.append(jnp.concatenate(terms, axis=1))

    def prepare(c):
        for j in range(2 * count):
            for t in range(RING):
                high, low = split(halves[j][pl.ds(t * cbd + c, half, stride=stride), :])
                for place_at, value in ((0, high), (1, low), (2, high)):
                    start = (3 * (j // 2) + place_at) * depth + (j % 2) * half
                    rhs[c, start : start + half, t * lanes : (t + 1) * lanes] = value

    def subtract(c):
        product = dot(left[min(c, 1)], rhs[c])
        for t in range(RING):
            at = pl.ds(t * cbd + c, rows, stride=stride)
            out_ref[at, :] = x_ref[at, :] - product[:, t * lanes : (t + 1) * lanes]

    first = (pl.program_id(0) == 0) & (pl.program_id(1) == 0)

    @pl.when(first)
    def _():
        prepare(0)
        for c in range(cbd):
            if c + 1 < cbd:
                prepare(c + 1)
            subtract(c)

    @pl.when(jnp.logical_not(first))
    def _():
        for c in range(cbd):
            subtract(c)


def subtract_products(lines, factors, ks, halves, cbd):
    nb = 2 * factors[0].shape[2]
    rbd = factors[0].shape[1] // nb
    count = len(halves) // 2
    tile = nb // SPLIT
    block = pl.BlockSpec((tile * RING * cbd, lines.shape[1]), lambda a, t, ks: (a * SPLIT + t, 0))
    parts = [
        pl.BlockSpec((1, tile, nb // 2), lambda a, t, ks, j=j: (ks[j], a * SPLIT + t, 0))
        for j in range(count)
        for _ in factors
    ]
    whole = [
        pl.BlockSpec(
            (nb // RING * RING * cbd, lines.shape[1]),
            lambda a, t, ks, i=i: (i, 0),
            pipeline_mode=pl.Buffered(buffer_count=1),
        )
        for _, i in halves
    ]
    return pl.pallas_call(
        functools.partial(update_kernel, count),
        grid_spec=pltpu.PrefetchScalarGridSpec(
            num_scalar_prefetch=1,
            grid=(rbd, SPLIT),
            in_specs=[block] + parts + whole,
            out_specs=block,
            scratch_shapes=[pltpu.VMEM((cbd, 3 * count * (nb // 2), nb), jnp.bfloat16)],
        ),
        out_shape=jax.ShapeDtypeStruct(lines.shape, lines.dtype),
        compiler_params=pltpu.CompilerParams(vmem_limit_bytes=VMEM_BYTES),
        cost_estimate=pl.CostEstimate(
            flops=3 * count * 11 * 10**8, bytes_accessed=(16 + 4 * count) * 2**20, transcendentals=0
        ),
    )(ks, lines, *(factors * count), *(t for t, _ in halves))


def column_kernel(x_ref, out_ref):
    rows, nb = out_ref.shape[1:]
    lanes = nb // RING
    cbd = x_ref.shape[0] // rows // RING
    for t in range(RING):
        at = pl.ds(t * cbd, rows, stride=RING * cbd)
        out_ref[0, :, t * lanes : (t + 1) * lanes] = x_ref[at, :]


def first_column(lines, rbd, nb, cbd):
    tile = nb // 2
    return pl.pallas_call(
        column_kernel,
        grid=(rbd, 2),
        in_specs=[pl.BlockSpec((tile * RING * cbd, lines.shape[1]), lambda a, t: (a * 2 + t, 0))],
        out_specs=pl.BlockSpec((1, tile, nb), lambda a, t: (a, t, 0)),
        out_shape=jax.ShapeDtypeStruct((rbd, nb, nb), lines.dtype),
        cost_estimate=pl.CostEstimate(flops=0, bytes_accessed=10 * 2**20, transcendentals=0),
    )(lines)


def corner_kernel(core_ref, x_ref, out_ref):
    half, nb = out_ref.shape
    lanes = nb // RING
    cbd = x_ref.shape[0] // nb // RING
    stride = RING * cbd

    @pl.when(core_ref[0] == 0)
    def _():
        for t in range(RING):
            out_ref[:, t * lanes : (t + 1) * lanes] = x_ref[pl.ds(t * cbd, half, stride=stride), :]

    @pl.when(core_ref[0] != 0)
    def _():
        for t in range(RING // 2):
            at = pl.ds((t + RING // 2) * cbd, nb, stride=stride)
            out_ref[t * lanes : (t + 1) * lanes, :] = x_ref[at, :].T


def corner_half(core, lines, nb, cbd):
    return pl.pallas_call(
        corner_kernel,
        grid=(1,),
        in_specs=[
            pl.BlockSpec(memory_space=pltpu.SMEM),
            pl.BlockSpec((nb * RING * cbd, lines.shape[1]), lambda i: (0, 0)),
        ],
        out_specs=pl.BlockSpec((nb // 2, nb), lambda i: (0, 0)),
        out_shape=jax.ShapeDtypeStruct((nb // 2, nb), lines.dtype),
        compiler_params=pltpu.CompilerParams(vmem_limit_bytes=VMEM_BYTES),
        cost_estimate=pl.CostEstimate(flops=0, bytes_accessed=5 * 2**20, transcendentals=0),
    )(core, lines)


def to_lines(matrix):
    rbd, rows, cbd, nb = matrix.shape
    cut = matrix.reshape(rbd, rows, cbd, RING, nb // RING)
    return cut.transpose(0, 1, 3, 2, 4).reshape(-1, nb // RING)


def from_lines(lines, shape):
    rbd, rows, cbd, nb = shape
    cut = lines.reshape(rbd, rows, RING, cbd, nb // RING)
    return cut.transpose(0, 1, 3, 2, 4).reshape(shape)


def share(x, index, first, second):
    one = send(x, first)
    two = send(jnp.where(index == 0, x, one), second)
    return choose(index, x, one, two, two)


def top_rows(lines, u, v, c):
    part = lines.shape[0] // 2 // RING
    small = part // RING

    def rows(k):
        return lax.dynamic_slice_in_dim(lines, (k % RING) * part, part)

    def root(z, y, x, c):
        return z == 0 and y < 2

    got = {d: send(rows(u + d), along_u(d, root)) for d in MOVES}
    own = rows(u)

    def quarter(d):
        begin = ((v + d) % RING) * small
        o, p, q, m = (
            lax.dynamic_slice_in_dim(t, begin, small) for t in (own, got[1], got[2], got[-1])
        )
        return jnp.stack([choose(u, o, p, q, m), choose(u, m, o, p, q)])

    def holder(z, y, x, c):
        return z == 0 if c == 0 else y < 2

    mine = quarter(0)
    sent = {d: send(quarter(d), along_v(d, holder)) for d in MOVES}
    part_a = choose(v, mine[0], sent[1][0], sent[2][0], sent[-1][0])
    part_b = jnp.where(
        c == 0,
        choose(v, mine[1], sent[1][1], sent[2][1], sent[-1][1]),
        choose(v, sent[-1][0], mine[0], sent[1][0], sent[2][0]),
    )
    piece = jnp.stack([part_a, part_b])
    whole = ring_order(v, piece, {d: send(piece, along_v(d)) for d in MOVES})

    before = send(whole, along_u(1))
    after = send(whole, along_u(-1))
    return whole, before, after


def row_inputs(column, start, u, v, x, c):
    def sign(c):
        return 1 if c == 0 else -1

    def x_first(z, y, x, c):
        return (z, y, sign(c), c) if x == 0 else None

    def x_second(z, y, x, c):
        if x == 0:
            return (z, y, -sign(c), c)
        return (z, y, 2, c) if x == sign(c) % RING else None

    s = jnp.where(c == 0, x, -x) % RING
    mine = share(column, s, pairs(x_first), pairs(x_second))
    def uv(z, y, c):
        return (y, z) if c == 0 else (z, y)

    def zyxc(u, v, x, c):
        return (v, u, x, c) if c == 0 else (u, v, x, c)

    def v_first(z, y, x, c):
        u, v = uv(z, y, c)
        return zyxc(u, 1, x, c) if x == 0 and v == 0 and u == 1 - c else None

    def v_second(z, y, x, c):
        u, v = uv(z, y, c)
        return zyxc(u, 3 if v == 0 else 2, x, c) if x == 0 and v < 2 and u == 1 - c else None

    def u_first(z, y, x, c):
        u, v = uv(z, y, c)
        return zyxc(u + 1, v, x, c) if x == 0 and u == 1 - c else None

    def u_second(z, y, x, c):
        u, v = uv(z, y, c)
        w = (u - 1 + c) % RING
        return zyxc(u - 1 if w == 0 else u + 1, v, x, c) if x == 0 and w < 2 else None

    line = share(start, v, pairs(v_first), pairs(v_second))
    plane = share(line, (u - 1 + c) % RING, pairs(u_first), pairs(u_second))
    here = share(plane, s, pairs(x_first), pairs(x_second))
    return mine, here


def body(matrix, inverse_factors):
    rbd, nb, cbd, _ = matrix.shape
    prow = lax.axis_index("row")
    pcol = lax.axis_index("col")
    z, y = prow // RING, prow % RING
    x, c = pcol // 2, pcol % 2
    u = jnp.where(c == 0, y, z)
    v = jnp.where(c == 0, z, y)

    lines = to_lines(matrix)
    own, before, after = top_rows(lines, u, v, c)
    start = corner_half(c.astype(jnp.int32)[None], lines, nb, cbd)
    mine, here = row_inputs(first_column(lines, rbd, nb, cbd), start, u, v, x, c)
    before, after, mine, turned = lax.optimization_barrier(
        (before, after, mine, weights(inverse_factors))
    )
    far = send(before[0], along_u(1)), send(after[1], along_u(-1))
    both = jnp.concatenate([mine.reshape(-1, nb), here])
    swapped = other_core(both)
    theirs, there = swapped[: rbd * nb].reshape(mine.shape), swapped[rbd * nb :]
    corner = jnp.concatenate([jnp.where(c == 0, here, there), jnp.where(c == 0, there, here)])

    where = jnp.stack([prow, pcol, c]).astype(jnp.int32)
    panels, *factors = row_factors(where, mine, theirs, corner, *turned)
    ks = jnp.stack([u, u - 1, u + 1, u + 2]).astype(jnp.int32) % RING
    far, factors = lax.optimization_barrier((far, factors))
    halves = [(t.reshape(-1, lines.shape[1]), i) for t in (own, before, after) for i in range(2)]
    halves += [(t, 0) for t in far]
    final = subtract_products(lines, factors, ks, halves, cbd)
    return panels, from_lines(final, matrix.shape)


def solution(mesh):
    return jax.shard_map(
        body,
        mesh=mesh,
        in_specs=(P(None, "row", None, "col"), P()),
        out_specs=(P(None, None, "row", None), P(None, "row", None, "col")),
        check_vma=False,
    )
```

```python
import functools

import jax
import jax.numpy as jnp
from jax import lax
from jax.experimental import pallas as pl
from jax.experimental.pallas import tpu as pltpu
from jax.sharding import PartitionSpec as P

AXES = ("row", "col")
RING = 4
MOVES = (1, -1, 2)
SPLIT = 2
VMEM_BYTES = 36 * 1024 * 1024
SMALL_VMEM_BYTES = 24 * 1024 * 1024


def place(z, y, x, c):
    return ((z % RING) * RING + y % RING) * (2 * RING) + (x % RING) * 2 + c


def pairs(target):
    found = []
    for z in range(RING):
        for y in range(RING):
            for x in range(RING):
                for c in range(2):
                    to = target(z, y, x, c)
                    if to is not None:
                        found.append((place(z, y, x, c), place(*to)))
    return found


def everyone(z, y, x, c):
    return True


def along_u(d, wanted=everyone):
    def target(z, y, x, c):
        if not wanted(z, y, x, c):
            return None
        return (z, y + d, x, c) if c == 0 else (z + d, y, x, c)

    return pairs(target)


def along_v(d, wanted=everyone):
    def target(z, y, x, c):
        if not wanted(z, y, x, c):
            return None
        return (z + d, y, x, c) if c == 0 else (z, y + d, x, c)

    return pairs(target)


def send(x, moves):
    return lax.ppermute(x, AXES, moves)


def other_core(x):
    return send(x, pairs(lambda z, y, x, c: (z, y, x, 1 - c)))


def choose(index, *options):
    result = options[-1]
    for i in range(len(options) - 2, -1, -1):
        result = jnp.where(index == i, options[i], result)
    return result


def ring_order(index, own, got):
    shape = (own.shape[0], RING) + own.shape[1:]
    whole = jnp.zeros(shape, own.dtype)
    for d, value in ((0, own), (-1, got[1]), (1, got[-1]), (2, got[2])):
        start = (0, (index + d) % RING) + (0,) * (len(shape) - 2)
        whole = lax.dynamic_update_slice(whole, value[:, None], start)
    return whole.reshape((own.shape[0], RING * own.shape[1]) + own.shape[2:])


def split(x):
    high = x.astype(jnp.bfloat16)
    low = (x - high.astype(jnp.float32)).astype(jnp.bfloat16)
    return high, low


def stack_left(x):
    high, low = split(x)
    return jnp.concatenate([high, high, low], axis=1)


def put_right(ref, columns, x):
    high, low = split(x)
    depth = x.shape[0]
    for i, value in enumerate((high, low, high)):
        ref[i * depth : (i + 1) * depth, columns] = value


def dot(a, b):
    return jnp.dot(a, b, preferred_element_type=jnp.float32)


def weights_kernel(inv_ref, first_ref, second_ref, right):
    nb = inv_ref.shape[1]
    for i, out_ref in enumerate((first_ref, second_ref)):
        inv = inv_ref[i]
        turned = inv.T
        put_right(right, slice(None), inv)
        put_right(out_ref, slice(0, nb), turned)
        put_right(out_ref, slice(nb, 2 * nb), dot(stack_left(turned), right[...]))


def weights(inverse_factors):
    _, nb, _ = inverse_factors.shape
    return pl.pallas_call(
        weights_kernel,
        out_shape=[jax.ShapeDtypeStruct((3 * nb, 2 * nb), jnp.bfloat16)] * 2,
        scratch_shapes=[pltpu.VMEM((3 * nb, nb), jnp.bfloat16)],
        compiler_params=pltpu.CompilerParams(vmem_limit_bytes=SMALL_VMEM_BYTES),
        cost_estimate=pl.CostEstimate(flops=2 * 10**9, bytes_accessed=8 * 2**20, transcendentals=0),
    )(inverse_factors)


def factors_kernel(
    where_ref, mine_ref, theirs_ref, corner_ref, first_ref, second_ref,
    panels_ref, yg_high, yg_low, ye_high, ye_low,
    f_turned, f_right,
):
    a = pl.program_id(0)
    prow, pcol, core = where_ref[0], where_ref[1], where_ref[2]
    part = yg_high.shape[2] // 2
    nb = mine_ref.shape[2]

    @pl.when((a == 0) & (pl.program_id(1) == 0))
    def _():
        f = dot(stack_left(corner_ref[...]), first_ref[:, nb:])
        put_right(f_right, slice(None), f)
        put_right(f_turned, slice(None), f.T)

    mine, theirs = mine_ref[0], theirs_ref[0]
    left = stack_left(jnp.where(core == 0, mine, theirs))
    right = jnp.where(core == 0, theirs, mine)
    block = a * 16 + prow
    panels_ref[0, 0] = dot(left, first_ref[:, :nb])
    z0 = jnp.where(block >= 1, dot(left, first_ref[:, nb:]), 0.0)
    below = stack_left(right - dot(left, f_turned[...]))
    panels_ref[1, 0] = jnp.where(block >= 1, dot(below, second_ref[:, :nb]), 0.0)
    y1 = jnp.where(block >= 2, dot(below, second_ref[:, nb:]), 0.0)
    y0 = z0 - dot(stack_left(y1), f_right[...])
    e0 = jnp.where(pcol == 0, 0.0, jnp.where(pcol == 1, z0, y0))
    e1 = jnp.where(pcol <= 1, 0.0, y1)
    for high, low, first, second in ((yg_high, yg_low, y0, y1), (ye_high, ye_low, e0, e1)):
        for i, value in enumerate((first, second)):
            h, l = split(value)
            for k in range(RING):
                high[k, :, i * part : (i + 1) * part] = h[:, k * part : (k + 1) * part]
                low[k, :, i * part : (i + 1) * part] = l[:, k * part : (k + 1) * part]


def row_factors(where, mine, theirs, corner, first, second):
    rbd, nb, _ = mine.shape
    tile = nb // SPLIT
    rows = pl.BlockSpec((1, tile, nb), lambda a, t: (a, t, 0))
    parts = pl.BlockSpec((RING, tile, nb // 2), lambda a, t: (0, a * SPLIT + t, 0))
    parts_shape = jax.ShapeDtypeStruct((RING, rbd * nb, nb // 2), jnp.bfloat16)
    fixed = [
        pl.BlockSpec(x.shape, lambda a, t: (0, 0), pipeline_mode=pl.Buffered(buffer_count=1))
        for x in (corner, first, second)
    ]
    return pl.pallas_call(
        factors_kernel,
        grid=(rbd, SPLIT),
        in_specs=[pl.BlockSpec(memory_space=pltpu.SMEM), rows, rows] + fixed,
        out_specs=[pl.BlockSpec((2, 1, tile, nb), lambda a, t: (0, a, t, 0))] + [parts] * 4,
        out_shape=[jax.ShapeDtypeStruct((2, rbd, nb, nb), jnp.float32)] + [parts_shape] * 4,
        scratch_shapes=[pltpu.VMEM((3 * nb, nb), jnp.bfloat16)] * 2,
        compiler_params=pltpu.CompilerParams(vmem_limit_bytes=SMALL_VMEM_BYTES),
        cost_estimate=pl.CostEstimate(flops=11 * 10**9, bytes_accessed=24 * 2**20, transcendentals=0),
    )(where, mine, theirs, corner, first, second)


def update_kernel(count, ks_ref, x_ref, *rest):
    factors, halves = rest[: 4 * count], rest[4 * count : 6 * count]
    out_ref, rhs = rest[6 * count], rest[6 * count + 1]
    rows, depth = factors[0].shape[1:]
    half = depth // 2
    cbd = rhs.shape[0]
    lanes = rhs.shape[2] // RING
    stride = RING * cbd

    left = []
    for kind in (1, 0):
        terms = []
        for j in range(count):
            h, l = factors[4 * j + 2 * kind][0], factors[4 * j + 2 * kind + 1][0]
            terms += [h, h, l]
        left.append(jnp.concatenate(terms, axis=1))

    def prepare(c):
        for j in range(2 * count):
            for t in range(RING):
                high, low = split(halves[j][pl.ds(t * cbd + c, half, stride=stride), :])
                for place_at, value in ((0, high), (1, low), (2, high)):
                    start = (3 * (j // 2) + place_at) * depth + (j % 2) * half
                    rhs[c, start : start + half, t * lanes : (t + 1) * lanes] = value

    def subtract(c):
        product = dot(left[min(c, 1)], rhs[c])
        for t in range(RING):
            at = pl.ds(t * cbd + c, rows, stride=stride)
            out_ref[at, :] = x_ref[at, :] - product[:, t * lanes : (t + 1) * lanes]

    first = (pl.program_id(0) == 0) & (pl.program_id(1) == 0)

    @pl.when(first)
    def _():
        prepare(0)
        for c in range(cbd):
            if c + 1 < cbd:
                prepare(c + 1)
            subtract(c)

    @pl.when(jnp.logical_not(first))
    def _():
        for c in range(cbd):
            subtract(c)


def subtract_products(lines, factors, ks, halves, cbd):
    nb = 2 * factors[0].shape[2]
    rbd = factors[0].shape[1] // nb
    count = len(halves) // 2
    tile = nb // SPLIT
    block = pl.BlockSpec((tile * RING * cbd, lines.shape[1]), lambda a, t, ks: (a * SPLIT + t, 0))
    parts = [
        pl.BlockSpec((1, tile, nb // 2), lambda a, t, ks, j=j: (ks[j], a * SPLIT + t, 0))
        for j in range(count)
        for _ in factors
    ]
    whole = [
        pl.BlockSpec(
            (nb // RING * RING * cbd, lines.shape[1]),
            lambda a, t, ks, i=i: (i, 0),
            pipeline_mode=pl.Buffered(buffer_count=1),
        )
        for _, i in halves
    ]
    return pl.pallas_call(
        functools.partial(update_kernel, count),
        grid_spec=pltpu.PrefetchScalarGridSpec(
            num_scalar_prefetch=1,
            grid=(rbd, SPLIT),
            in_specs=[block] + parts + whole,
            out_specs=block,
            scratch_shapes=[pltpu.VMEM((cbd, 3 * count * (nb // 2), nb), jnp.bfloat16)],
        ),
        out_shape=jax.ShapeDtypeStruct(lines.shape, lines.dtype),
        compiler_params=pltpu.CompilerParams(vmem_limit_bytes=VMEM_BYTES),
        cost_estimate=pl.CostEstimate(
            flops=3 * count * 11 * 10**8, bytes_accessed=(16 + 4 * count) * 2**20, transcendentals=0
        ),
    )(ks, lines, *(factors * count), *(t for t, _ in halves))


def column_kernel(x_ref, out_ref):
    rows, nb = out_ref.shape[1:]
    lanes = nb // RING
    cbd = x_ref.shape[0] // rows // RING
    for t in range(RING):
        at = pl.ds(t * cbd, rows, stride=RING * cbd)
        out_ref[0, :, t * lanes : (t + 1) * lanes] = x_ref[at, :]


def first_column(lines, rbd, nb, cbd):
    tile = nb // 2
    return pl.pallas_call(
        column_kernel,
        grid=(rbd, 2),
        in_specs=[pl.BlockSpec((tile * RING * cbd, lines.shape[1]), lambda a, t: (a * 2 + t, 0))],
        out_specs=pl.BlockSpec((1, tile, nb), lambda a, t: (a, t, 0)),
        out_shape=jax.ShapeDtypeStruct((rbd, nb, nb), lines.dtype),
        cost_estimate=pl.CostEstimate(flops=0, bytes_accessed=10 * 2**20, transcendentals=0),
    )(lines)


def corner_kernel(core_ref, x_ref, out_ref):
    half, nb = out_ref.shape
    lanes = nb // RING
    cbd = x_ref.shape[0] // nb // RING
    stride = RING * cbd

    @pl.when(core_ref[0] == 0)
    def _():
        for t in range(RING):
            out_ref[:, t * lanes : (t + 1) * lanes] = x_ref[pl.ds(t * cbd, half, stride=stride), :]

    @pl.when(core_ref[0] != 0)
    def _():
        for t in range(RING // 2):
            at = pl.ds((t + RING // 2) * cbd, nb, stride=stride)
            out_ref[t * lanes : (t + 1) * lanes, :] = x_ref[at, :].T


def corner_half(core, lines, nb, cbd):
    return pl.pallas_call(
        corner_kernel,
        grid=(1,),
        in_specs=[
            pl.BlockSpec(memory_space=pltpu.SMEM),
            pl.BlockSpec((nb * RING * cbd, lines.shape[1]), lambda i: (0, 0)),
        ],
        out_specs=pl.BlockSpec((nb // 2, nb), lambda i: (0, 0)),
        out_shape=jax.ShapeDtypeStruct((nb // 2, nb), lines.dtype),
        compiler_params=pltpu.CompilerParams(vmem_limit_bytes=SMALL_VMEM_BYTES),
        cost_estimate=pl.CostEstimate(flops=0, bytes_accessed=5 * 2**20, transcendentals=0),
    )(core, lines)


def to_lines(matrix):
    rbd, rows, cbd, nb = matrix.shape
    cut = matrix.reshape(rbd, rows, cbd, RING, nb // RING)
    return cut.transpose(0, 1, 3, 2, 4).reshape(-1, nb // RING)


def from_lines(lines, shape):
    rbd, rows, cbd, nb = shape
    cut = lines.reshape(rbd, rows, RING, cbd, nb // RING)
    return cut.transpose(0, 1, 3, 2, 4).reshape(shape)


def share(x, index, first, second):
    one = send(x, first)
    two = send(jnp.where(index == 0, x, one), second)
    return choose(index, x, one, two, two)


def top_rows(lines, u, v, c):
    part = lines.shape[0] // 2 // RING
    small = part // RING

    def rows(k):
        return lax.dynamic_slice_in_dim(lines, (k % RING) * part, part)

    def root(z, y, x, c):
        return z == 0 and y < 2

    got = {d: send(rows(u + d), along_u(d, root)) for d in MOVES}
    own = rows(u)

    def quarter(d):
        begin = ((v + d) % RING) * small
        o, p, q, m = (
            lax.dynamic_slice_in_dim(t, begin, small) for t in (own, got[1], got[2], got[-1])
        )
        return jnp.stack([choose(u, o, p, q, m), choose(u, m, o, p, q)])

    def holder(z, y, x, c):
        return z == 0 if c == 0 else y < 2

    mine = quarter(0)
    sent = {d: send(quarter(d), along_v(d, holder)) for d in MOVES}
    part_a = choose(v, mine[0], sent[1][0], sent[2][0], sent[-1][0])
    part_b = jnp.where(
        c == 0,
        choose(v, mine[1], sent[1][1], sent[2][1], sent[-1][1]),
        choose(v, sent[-1][0], mine[0], sent[1][0], sent[2][0]),
    )
    piece = jnp.stack([part_a, part_b])
    whole = ring_order(v, piece, {d: send(piece, along_v(d)) for d in MOVES})

    before = send(whole, along_u(1))
    after = send(whole, along_u(-1))
    return whole, before, after


def row_inputs(column, start, u, v, x, c):
    def sign(c):
        return 1 if c == 0 else -1

    def x_first(z, y, x, c):
        return (z, y, sign(c), c) if x == 0 else None

    def x_second(z, y, x, c):
        if x == 0:
            return (z, y, -sign(c), c)
        return (z, y, 2, c) if x == sign(c) % RING else None

    s = jnp.where(c == 0, x, -x) % RING
    mine = share(column, s, pairs(x_first), pairs(x_second))
    def uv(z, y, c):
        return (y, z) if c == 0 else (z, y)

    def zyxc(u, v, x, c):
        return (v, u, x, c) if c == 0 else (u, v, x, c)

    def v_first(z, y, x, c):
        u, v = uv(z, y, c)
        return zyxc(u, 1, x, c) if x == 0 and v == 0 and u == 1 - c else None

    def v_second(z, y, x, c):
        u, v = uv(z, y, c)
        return zyxc(u, 3 if v == 0 else 2, x, c) if x == 0 and v < 2 and u == 1 - c else None

    def u_first(z, y, x, c):
        u, v = uv(z, y, c)
        return zyxc(u + 1, v, x, c) if x == 0 and u == 1 - c else None

    def u_second(z, y, x, c):
        u, v = uv(z, y, c)
        w = (u - 1 + c) % RING
        return zyxc(u - 1 if w == 0 else u + 1, v, x, c) if x == 0 and w < 2 else None

    line = share(start, v, pairs(v_first), pairs(v_second))
    plane = share(line, (u - 1 + c) % RING, pairs(u_first), pairs(u_second))
    here = share(plane, s, pairs(x_first), pairs(x_second))
    return mine, here


def body(matrix, inverse_factors):
    rbd, nb, cbd, _ = matrix.shape
    prow = lax.axis_index("row")
    pcol = lax.axis_index("col")
    z, y = prow // RING, prow % RING
    x, c = pcol // 2, pcol % 2
    u = jnp.where(c == 0, y, z)
    v = jnp.where(c == 0, z, y)

    lines = to_lines(matrix)
    own, before, after = top_rows(lines, u, v, c)
    start = corner_half(c.astype(jnp.int32)[None], lines, nb, cbd)
    mine, here = row_inputs(first_column(lines, rbd, nb, cbd), start, u, v, x, c)
    before, after, mine, turned = lax.optimization_barrier(
        (before, after, mine, weights(inverse_factors))
    )
    far = send(before[0], along_u(1)), send(after[1], along_u(-1))
    both = jnp.concatenate([mine.reshape(-1, nb), here])
    swapped = other_core(both)
    theirs, there = swapped[: rbd * nb].reshape(mine.shape), swapped[rbd * nb :]
    corner = jnp.concatenate([jnp.where(c == 0, here, there), jnp.where(c == 0, there, here)])

    where = jnp.stack([prow, pcol, c]).astype(jnp.int32)
    panels, *factors = row_factors(where, mine, theirs, corner, *turned)
    ks = jnp.stack([u, u - 1, u + 1, u + 2]).astype(jnp.int32) % RING
    far, factors = lax.optimization_barrier((far, factors))
    halves = [(t.reshape(-1, lines.shape[1]), i) for t in (own, before, after) for i in range(2)]
    halves += [(t, 0) for t in far]
    final = subtract_products(lines, factors, ks, halves, cbd)
    return panels, from_lines(final, matrix.shape)


def solution(mesh):
    return jax.shard_map(
        body,
        mesh=mesh,
        in_specs=(P(None, "row", None, "col"), P()),
        out_specs=(P(None, None, "row", None), P(None, "row", None, "col")),
        check_vma=False,
    )
```

```python
import functools

import jax
import jax.numpy as jnp
from jax import lax
from jax.experimental import pallas as pl
from jax.experimental.pallas import tpu as pltpu
from jax.sharding import PartitionSpec as P

AXES = ("row", "col")
RING = 4
MOVES = (1, -1, 2)
SPLIT = 2
VMEM_BYTES = 36 * 1024 * 1024
SMALL_VMEM_BYTES = 24 * 1024 * 1024
EARLY_VMEM_BYTES = 16 * 1024 * 1024


def place(z, y, x, c):
    return ((z % RING) * RING + y % RING) * (2 * RING) + (x % RING) * 2 + c


def pairs(target):
    found = []
    for z in range(RING):
        for y in range(RING):
            for x in range(RING):
                for c in range(2):
                    to = target(z, y, x, c)
                    if to is not None:
                        found.append((place(z, y, x, c), place(*to)))
    return found


def everyone(z, y, x, c):
    return True


def along_u(d, wanted=everyone):
    def target(z, y, x, c):
        if not wanted(z, y, x, c):
            return None
        return (z, y + d, x, c) if c == 0 else (z + d, y, x, c)

    return pairs(target)


def along_v(d, wanted=everyone):
    def target(z, y, x, c):
        if not wanted(z, y, x, c):
            return None
        return (z + d, y, x, c) if c == 0 else (z, y + d, x, c)

    return pairs(target)


def send(x, moves):
    return lax.ppermute(x, AXES, moves)


def other_core(x):
    return send(x, pairs(lambda z, y, x, c: (z, y, x, 1 - c)))


def choose(index, *options):
    result = options[-1]
    for i in range(len(options) - 2, -1, -1):
        result = jnp.where(index == i, options[i], result)
    return result


def ring_order(index, own, got):
    shape = (own.shape[0], RING) + own.shape[1:]
    whole = jnp.zeros(shape, own.dtype)
    for d, value in ((0, own), (-1, got[1]), (1, got[-1]), (2, got[2])):
        start = (0, (index + d) % RING) + (0,) * (len(shape) - 2)
        whole = lax.dynamic_update_slice(whole, value[:, None], start)
    return whole.reshape((own.shape[0], RING * own.shape[1]) + own.shape[2:])


def split(x):
    high = x.astype(jnp.bfloat16)
    low = (x - high.astype(jnp.float32)).astype(jnp.bfloat16)
    return high, low


def stack_left(x):
    high, low = split(x)
    return jnp.concatenate([high, high, low], axis=1)


def put_right(ref, columns, x):
    high, low = split(x)
    depth = x.shape[0]
    for i, value in enumerate((high, low, high)):
        ref[i * depth : (i + 1) * depth, columns] = value


def dot(a, b):
    return jnp.dot(a, b, preferred_element_type=jnp.float32)


def weights_kernel(inv_ref, first_ref, second_ref, right):
    nb = inv_ref.shape[1]
    for i, out_ref in enumerate((first_ref, second_ref)):
        inv = inv_ref[i]
        turned = inv.T
        put_right(right, slice(None), inv)
        put_right(out_ref, slice(0, nb), turned)
        put_right(out_ref, slice(nb, 2 * nb), dot(stack_left(turned), right[...]))


def weights(inverse_factors):
    _, nb, _ = inverse_factors.shape
    return pl.pallas_call(
        weights_kernel,
        out_shape=[jax.ShapeDtypeStruct((3 * nb, 2 * nb), jnp.bfloat16)] * 2,
        scratch_shapes=[pltpu.VMEM((3 * nb, nb), jnp.bfloat16)],
        compiler_params=pltpu.CompilerParams(vmem_limit_bytes=EARLY_VMEM_BYTES),
        cost_estimate=pl.CostEstimate(flops=2 * 10**9, bytes_accessed=8 * 2**20, transcendentals=0),
    )(inverse_factors)


def factors_kernel(
    where_ref, mine_ref, theirs_ref, corner_ref, first_ref, second_ref,
    panels_ref, yg_high, yg_low, ye_high, ye_low,
    f_turned, f_right,
):
    a = pl.program_id(0)
    prow, pcol, core = where_ref[0], where_ref[1], where_ref[2]
    part = yg_high.shape[2] // 2
    nb = mine_ref.shape[2]

    @pl.when((a == 0) & (pl.program_id(1) == 0))
    def _():
        f = dot(stack_left(corner_ref[...]), first_ref[:, nb:])
        put_right(f_right, slice(None), f)
        put_right(f_turned, slice(None), f.T)

    mine, theirs = mine_ref[0], theirs_ref[0]
    left = stack_left(jnp.where(core == 0, mine, theirs))
    right = jnp.where(core == 0, theirs, mine)
    block = a * 16 + prow
    panels_ref[0, 0] = dot(left, first_ref[:, :nb])
    z0 = jnp.where(block >= 1, dot(left, first_ref[:, nb:]), 0.0)
    below = stack_left(right - dot(left, f_turned[...]))
    panels_ref[1, 0] = jnp.where(block >= 1, dot(below, second_ref[:, :nb]), 0.0)
    y1 = jnp.where(block >= 2, dot(below, second_ref[:, nb:]), 0.0)
    y0 = z0 - dot(stack_left(y1), f_right[...])
    e0 = jnp.where(pcol == 0, 0.0, jnp.where(pcol == 1, z0, y0))
    e1 = jnp.where(pcol <= 1, 0.0, y1)
    for high, low, first, second in ((yg_high, yg_low, y0, y1), (ye_high, ye_low, e0, e1)):
        for i, value in enumerate((first, second)):
            h, l = split(value)
            for k in range(RING):
                high[k, :, i * part : (i + 1) * part] = h[:, k * part : (k + 1) * part]
                low[k, :, i * part : (i + 1) * part] = l[:, k * part : (k + 1) * part]


def row_factors(where, mine, theirs, corner, first, second):
    rbd, nb, _ = mine.shape
    tile = nb // SPLIT
    rows = pl.BlockSpec((1, tile, nb), lambda a, t: (a, t, 0))
    parts = pl.BlockSpec((RING, tile, nb // 2), lambda a, t: (0, a * SPLIT + t, 0))
    parts_shape = jax.ShapeDtypeStruct((RING, rbd * nb, nb // 2), jnp.bfloat16)
    fixed = [
        pl.BlockSpec(x.shape, lambda a, t: (0, 0), pipeline_mode=pl.Buffered(buffer_count=1))
        for x in (corner, first, second)
    ]
    return pl.pallas_call(
        factors_kernel,
        grid=(rbd, SPLIT),
        in_specs=[pl.BlockSpec(memory_space=pltpu.SMEM), rows, rows] + fixed,
        out_specs=[pl.BlockSpec((2, 1, tile, nb), lambda a, t: (0, a, t, 0))] + [parts] * 4,
        out_shape=[jax.ShapeDtypeStruct((2, rbd, nb, nb), jnp.float32)] + [parts_shape] * 4,
        scratch_shapes=[pltpu.VMEM((3 * nb, nb), jnp.bfloat16)] * 2,
        compiler_params=pltpu.CompilerParams(vmem_limit_bytes=SMALL_VMEM_BYTES),
        cost_estimate=pl.CostEstimate(flops=11 * 10**9, bytes_accessed=24 * 2**20, transcendentals=0),
    )(where, mine, theirs, corner, first, second)


def update_kernel(count, ks_ref, x_ref, *rest):
    factors, halves = rest[: 4 * count], rest[4 * count : 6 * count]
    out_ref, rhs = rest[6 * count], rest[6 * count + 1]
    rows, depth = factors[0].shape[1:]
    half = depth // 2
    cbd = rhs.shape[0]
    lanes = rhs.shape[2] // RING
    stride = RING * cbd

    left = []
    for kind in (1, 0):
        terms = []
        for j in range(count):
            h, l = factors[4 * j + 2 * kind][0], factors[4 * j + 2 * kind + 1][0]
            terms += [h, h, l]
        left.append(jnp.concatenate(terms, axis=1))

    def prepare(c):
        for j in range(2 * count):
            for t in range(RING):
                high, low = split(halves[j][pl.ds(t * cbd + c, half, stride=stride), :])
                for place_at, value in ((0, high), (1, low), (2, high)):
                    start = (3 * (j // 2) + place_at) * depth + (j % 2) * half
                    rhs[c, start : start + half, t * lanes : (t + 1) * lanes] = value

    def subtract(c):
        product = dot(left[min(c, 1)], rhs[c])
        for t in range(RING):
            at = pl.ds(t * cbd + c, rows, stride=stride)
            out_ref[at, :] = x_ref[at, :] - product[:, t * lanes : (t + 1) * lanes]

    first = (pl.program_id(0) == 0) & (pl.program_id(1) == 0)

    @pl.when(first)
    def _():
        prepare(0)
        for c in range(cbd):
            if c + 1 < cbd:
                prepare(c + 1)
            subtract(c)

    @pl.when(jnp.logical_not(first))
    def _():
        for c in range(cbd):
            subtract(c)


def subtract_products(lines, factors, ks, halves, cbd):
    nb = 2 * factors[0].shape[2]
    rbd = factors[0].shape[1] // nb
    count = len(halves) // 2
    tile = nb // SPLIT
    block = pl.BlockSpec((tile * RING * cbd, lines.shape[1]), lambda a, t, ks: (a * SPLIT + t, 0))
    parts = [
        pl.BlockSpec((1, tile, nb // 2), lambda a, t, ks, j=j: (ks[j], a * SPLIT + t, 0))
        for j in range(count)
        for _ in factors
    ]
    whole = [
        pl.BlockSpec(
            (nb // RING * RING * cbd, lines.shape[1]),
            lambda a, t, ks, i=i: (i, 0),
            pipeline_mode=pl.Buffered(buffer_count=1),
        )
        for _, i in halves
    ]
    return pl.pallas_call(
        functools.partial(update_kernel, count),
        grid_spec=pltpu.PrefetchScalarGridSpec(
            num_scalar_prefetch=1,
            grid=(rbd, SPLIT),
            in_specs=[block] + parts + whole,
            out_specs=block,
            scratch_shapes=[pltpu.VMEM((cbd, 3 * count * (nb // 2), nb), jnp.bfloat16)],
        ),
        out_shape=jax.ShapeDtypeStruct(lines.shape, lines.dtype),
        compiler_params=pltpu.CompilerParams(vmem_limit_bytes=VMEM_BYTES),
        cost_estimate=pl.CostEstimate(
            flops=3 * count * 11 * 10**8, bytes_accessed=(16 + 4 * count) * 2**20, transcendentals=0
        ),
    )(ks, lines, *(factors * count), *(t for t, _ in halves))


def column_kernel(x_ref, out_ref):
    rows, nb = out_ref.shape[1:]
    lanes = nb // RING
    cbd = x_ref.shape[0] // rows // RING
    for t in range(RING):
        at = pl.ds(t * cbd, rows, stride=RING * cbd)
        out_ref[0, :, t * lanes : (t + 1) * lanes] = x_ref[at, :]


def first_column(lines, rbd, nb, cbd):
    tile = nb // 2
    return pl.pallas_call(
        column_kernel,
        grid=(rbd, 2),
        in_specs=[pl.BlockSpec((tile * RING * cbd, lines.shape[1]), lambda a, t: (a * 2 + t, 0))],
        out_specs=pl.BlockSpec((1, tile, nb), lambda a, t: (a, t, 0)),
        out_shape=jax.ShapeDtypeStruct((rbd, nb, nb), lines.dtype),
        cost_estimate=pl.CostEstimate(flops=0, bytes_accessed=10 * 2**20, transcendentals=0),
    )(lines)


def corner_kernel(core_ref, x_ref, out_ref):
    half, nb = out_ref.shape
    lanes = nb // RING
    cbd = x_ref.shape[0] // nb // RING
    stride = RING * cbd

    @pl.when(core_ref[0] == 0)
    def _():
        for t in range(RING):
            out_ref[:, t * lanes : (t + 1) * lanes] = x_ref[pl.ds(t * cbd, half, stride=stride), :]

    @pl.when(core_ref[0] != 0)
    def _():
        for t in range(RING // 2):
            at = pl.ds((t + RING // 2) * cbd, nb, stride=stride)
            out_ref[t * lanes : (t + 1) * lanes, :] = x_ref[at, :].T


def corner_half(core, lines, nb, cbd):
    return pl.pallas_call(
        corner_kernel,
        grid=(1,),
        in_specs=[
            pl.BlockSpec(memory_space=pltpu.SMEM),
            pl.BlockSpec((nb * RING * cbd, lines.shape[1]), lambda i: (0, 0)),
        ],
        out_specs=pl.BlockSpec((nb // 2, nb), lambda i: (0, 0)),
        out_shape=jax.ShapeDtypeStruct((nb // 2, nb), lines.dtype),
        compiler_params=pltpu.CompilerParams(vmem_limit_bytes=EARLY_VMEM_BYTES),
        cost_estimate=pl.CostEstimate(flops=0, bytes_accessed=5 * 2**20, transcendentals=0),
    )(core, lines)


def to_lines(matrix):
    rbd, rows, cbd, nb = matrix.shape
    cut = matrix.reshape(rbd, rows, cbd, RING, nb // RING)
    return cut.transpose(0, 1, 3, 2, 4).reshape(-1, nb // RING)


def from_lines(lines, shape):
    rbd, rows, cbd, nb = shape
    cut = lines.reshape(rbd, rows, RING, cbd, nb // RING)
    return cut.transpose(0, 1, 3, 2, 4).reshape(shape)


def share(x, index, first, second):
    one = send(x, first)
    two = send(jnp.where(index == 0, x, one), second)
    return choose(index, x, one, two, two)


def top_rows(lines, u, v, c):
    part = lines.shape[0] // 2 // RING
    small = part // RING

    def rows(k):
        return lax.dynamic_slice_in_dim(lines, (k % RING) * part, part)

    def root(z, y, x, c):
        return z == 0 and y < 2

    got = {d: send(rows(u + d), along_u(d, root)) for d in MOVES}
    own = rows(u)

    def quarter(d):
        begin = ((v + d) % RING) * small
        o, p, q, m = (
            lax.dynamic_slice_in_dim(t, begin, small) for t in (own, got[1], got[2], got[-1])
        )
        return jnp.stack([choose(u, o, p, q, m), choose(u, m, o, p, q)])

    def holder(z, y, x, c):
        return z == 0 if c == 0 else y < 2

    mine = quarter(0)
    sent = {d: send(quarter(d), along_v(d, holder)) for d in MOVES}
    part_a = choose(v, mine[0], sent[1][0], sent[2][0], sent[-1][0])
    part_b = jnp.where(
        c == 0,
        choose(v, mine[1], sent[1][1], sent[2][1], sent[-1][1]),
        choose(v, sent[-1][0], mine[0], sent[1][0], sent[2][0]),
    )
    piece = jnp.stack([part_a, part_b])
    whole = ring_order(v, piece, {d: send(piece, along_v(d)) for d in MOVES})

    before = send(whole, along_u(1))
    after = send(whole, along_u(-1))
    return whole, before, after


def row_inputs(column, start, u, v, x, c):
    def sign(c):
        return 1 if c == 0 else -1

    def x_first(z, y, x, c):
        return (z, y, sign(c), c) if x == 0 else None

    def x_second(z, y, x, c):
        if x == 0:
            return (z, y, -sign(c), c)
        return (z, y, 2, c) if x == sign(c) % RING else None

    s = jnp.where(c == 0, x, -x) % RING
    mine = share(column, s, pairs(x_first), pairs(x_second))
    def uv(z, y, c):
        return (y, z) if c == 0 else (z, y)

    def zyxc(u, v, x, c):
        return (v, u, x, c) if c == 0 else (u, v, x, c)

    def v_first(z, y, x, c):
        u, v = uv(z, y, c)
        return zyxc(u, 1, x, c) if x == 0 and v == 0 and u == 1 - c else None

    def v_second(z, y, x, c):
        u, v = uv(z, y, c)
        return zyxc(u, 3 if v == 0 else 2, x, c) if x == 0 and v < 2 and u == 1 - c else None

    def u_first(z, y, x, c):
        u, v = uv(z, y, c)
        return zyxc(u + 1, v, x, c) if x == 0 and u == 1 - c else None

    def u_second(z, y, x, c):
        u, v = uv(z, y, c)
        w = (u - 1 + c) % RING
        return zyxc(u - 1 if w == 0 else u + 1, v, x, c) if x == 0 and w < 2 else None

    line = share(start, v, pairs(v_first), pairs(v_second))
    plane = share(line, (u - 1 + c) % RING, pairs(u_first), pairs(u_second))
    here = share(plane, s, pairs(x_first), pairs(x_second))
    return mine, here


def body(matrix, inverse_factors):
    rbd, nb, cbd, _ = matrix.shape
    prow = lax.axis_index("row")
    pcol = lax.axis_index("col")
    z, y = prow // RING, prow % RING
    x, c = pcol // 2, pcol % 2
    u = jnp.where(c == 0, y, z)
    v = jnp.where(c == 0, z, y)

    lines = to_lines(matrix)
    own, before, after = top_rows(lines, u, v, c)
    start = corner_half(c.astype(jnp.int32)[None], lines, nb, cbd)
    mine, here = row_inputs(first_column(lines, rbd, nb, cbd), start, u, v, x, c)
    before, after, mine, turned = lax.optimization_barrier(
        (before, after, mine, weights(inverse_factors))
    )
    far = send(before[0], along_u(1)), send(after[1], along_u(-1))
    both = jnp.concatenate([mine.reshape(-1, nb), here])
    swapped = other_core(both)
    theirs, there = swapped[: rbd * nb].reshape(mine.shape), swapped[rbd * nb :]
    corner = jnp.concatenate([jnp.where(c == 0, here, there), jnp.where(c == 0, there, here)])

    where = jnp.stack([prow, pcol, c]).astype(jnp.int32)
    panels, *factors = row_factors(where, mine, theirs, corner, *turned)
    ks = jnp.stack([u, u - 1, u + 1, u + 2]).astype(jnp.int32) % RING
    far, factors = lax.optimization_barrier((far, factors))
    halves = [(t.reshape(-1, lines.shape[1]), i) for t in (own, before, after) for i in range(2)]
    halves += [(t, 0) for t in far]
    final = subtract_products(lines, factors, ks, halves, cbd)
    return panels, from_lines(final, matrix.shape)


def solution(mesh):
    return jax.shard_map(
        body,
        mesh=mesh,
        in_specs=(P(None, "row", None, "col"), P()),
        out_specs=(P(None, None, "row", None), P(None, "row", None, "col")),
        check_vma=False,
    )
```
